32 devices in a mesh: groups: 2 (over y), lat: 4 (over z), chan: 2 (over x), lon: 2 (over core).
Axes of the slice: x: 2, y: 2, z: 4, core: 2. Of those that a mesh axis runs over, the one named last changes fastest.
Arguments:
- field_in: bfloat16 [1440, 24, 640], P(('groups', 'lon'), ('lat', 'chan')), parts along dimension 0, may hold values from -6 to 6
- cotangent: bfloat16 [1440, 24, 640], P(('groups', 'lon'), ('lat', 'chan')), parts along dimension 0, may hold values from -6 to 6
- mlp_in_weight: bfloat16 [640, 640], P('chan'), may hold values from -0.25 to 0.25
- mlp_out_weight: bfloat16 [640, 640], P('chan'), may hold values from -0.25 to 0.25
- legendre_analysis: bfloat16 [2, 128, 240, 24], P('lon', ('lat', 'chan')), may hold values from -1.25 to 1.25
- legendre_synthesis: bfloat16 [2, 128, 24, 240], P('lon', ('lat', 'chan')), may hold values from -0.375 to 0.375
- spectral_gain: bfloat16 [240, 640], replicated, may hold values from -1.5 to 1.5
- disco_filter: bfloat16 [120, 2, 256], P(('lat', 'chan'), None, 'lon'), may hold values from -3 to 3
- slot_pairs: int32 [120, 2], P(('lat', 'chan')), may hold values from 0 to 4, as said below
- slot_count: int32 [8], P(('lat', 'chan')), may hold values from 9 to 15
Outputs:
- field_grad: bfloat16 [1440, 24, 640], P(('groups', 'lon'), ('lat', 'chan')), parts along dimension 0
The draws below stay inside these ranges and needn't reach their ends.
There are 2 independent parts, one for each index of `groups`. The reference program is written for one: setup_inputs(seed, part) draws one part's arguments, and reference() takes and returns one part's arrays. A program takes and returns all parts, laid end to end along the dimension named above; an argument that names none is the same for every part. Nothing has to cross between parts.
Inputs may be any that keep to these rules, and one draw needn't show every extreme that they name: `slot_pairs`: slots b * 15 to b * 15 + 14 belong to band b. A slot holds an output row r within the band (first entry, below 3) and an offset q of 0 to 2 * 2 (second entry): its input row lies q - 2 rows from the output row, within the band's window of 7 rows that begins 2 rows before the band. Among the first slot_count[b] slots of a band no pair repeats; the band's later slots are not used.
All inputs are finite; a program needn't handle non-finite values.
Results may differ from the reference program's by a relative error of at most 0.01.
Values may be sent and summed in bfloat16 or wider, within the bound.
A program may use at most 64 MiB of HBM per device.

```python
import math
import jax
import jax.numpy as jnp

C = 640
HID = 640
NLON = 720
MODES = 256
DEG = 240
LAT_DEV = 3
REACH = 2
BANDS = 8
NLAT = 24
SLOT_MAX = 15
N_LON = 2


def slot_layout(key):
    polar_key, order_key = jax.random.split(key)
    polar_bands = jax.random.randint(polar_key, (), max(1, BANDS // 8), max(1, BANDS // 4) + 1)
    band_ids = jnp.arange(BANDS, dtype=jnp.int32)
    near_pole = (band_ids < polar_bands) | (band_ids >= BANDS - polar_bands)
    band_reach = jnp.where(near_pole, REACH, 1).astype(jnp.int32)
    stencil_width = 2 * REACH + 1
    slot_ids = jnp.arange(SLOT_MAX, dtype=jnp.int32)
    slot_rows = slot_ids // stencil_width
    slot_offsets = slot_ids % stencil_width - REACH
    in_use = jnp.abs(slot_offsets)[None, :] <= band_reach[:, None]
    shuffled = jax.vmap(lambda sub_key: jax.random.permutation(sub_key, SLOT_MAX))(jax.random.split(order_key, BANDS))
    sort_keys = jnp.where(in_use, 0, SLOT_MAX) + shuffled.astype(jnp.int32)
    slot_order = jnp.argsort(sort_keys, axis=1)
    pair_rows = slot_rows[slot_order]
    pair_cols = slot_offsets[slot_order] + REACH
    pairs_all = jnp.stack([pair_rows, pair_cols], axis=-1).reshape(BANDS * SLOT_MAX, 2).astype(jnp.int32)
    counts_all = (LAT_DEV * (2 * band_reach + 1)).astype(jnp.int32)
    return (pairs_all, counts_all)


def draw_slot_pairs(key, part):
    return slot_layout(key)[0]


def draw_slot_count(key, part):
    return slot_layout(key)[1]


def steps_of(own_key, extent, shards, smallest, largest):
    def one(dim, blocks):
        steps = jax.random.uniform(jax.random.fold_in(jax.random.fold_in(own_key, 6), dim), (blocks,), jnp.float32, smallest / len(shards), largest / len(shards))
        return jnp.repeat(jnp.exp(steps), extent[dim] // blocks).reshape((-1,) + (1,) * (len(extent) - dim - 1))

    factor_of = one(*shards[0])
    for cut in shards[1:]:
        factor_of = factor_of * one(*cut)
    return factor_of


def scatter_about(stream_key, shape, scale, limit, cuts=(), held_as=jnp.bfloat16):
    level = steps_of(stream_key, shape, cuts, -0.22, 0.18) if cuts else 1.0
    values = jax.random.normal(stream_key, shape, jnp.float32) * scale * level
    return jnp.minimum(jnp.maximum(values, -limit), limit).astype(held_as)


def setup_inputs(seed: int = 0, part: int = 0) -> dict:
    keys = jax.random.split(jax.random.key(seed), 11)
    part_splits = jax.random.split(jax.random.fold_in(keys[10], part), 11)
    field_in = scatter_about(part_splits[0], (NLON, NLAT, C), 1.0, 6.0, ((0, 2), (1, 8)))
    cotangent = scatter_about(part_splits[1], (NLON, NLAT, C), 1.0, 6.0, ((0, 2), (1, 8)))
    mlp_in_weight = scatter_about(keys[2], (C, HID), C ** -0.5, 0.25, ((0, 2),))
    mlp_out_weight = scatter_about(keys[3], (HID, C), HID ** -0.5, 0.25, ((0, 2),))
    legendre_analysis = scatter_about(keys[4], (N_LON, MODES // N_LON, DEG, NLAT), NLAT ** -0.5, 1.25, ((0, 2), (1, 8)))
    legendre_synthesis = scatter_about(keys[5], (N_LON, MODES // N_LON, NLAT, DEG), DEG ** -0.5, 0.375, ((0, 2), (1, 8)))
    spectral_gain = jnp.clip(jax.random.uniform(keys[6], (DEG, C), jnp.float32, -1.5, 1.5), -1.5, 1.5).astype(jnp.bfloat16)
    disco_filter = scatter_about(keys[7], (BANDS * SLOT_MAX, 2, MODES), 0.5, 3.0, ((0, 8), (2, 2)))
    slot_pairs = draw_slot_pairs(jax.random.fold_in(keys[10], 71), part)
    slot_count = draw_slot_count(jax.random.fold_in(keys[10], 71), part)
    return dict(field_in=field_in, cotangent=cotangent, mlp_in_weight=mlp_in_weight, mlp_out_weight=mlp_out_weight, legendre_analysis=legendre_analysis, legendre_synthesis=legendre_synthesis, spectral_gain=spectral_gain, disco_filter=disco_filter, slot_pairs=slot_pairs, slot_count=slot_count)


def gelu_slope(inputs):
    normal_cdf = 0.5 * (1.0 + jax.scipy.special.erf(inputs * (1.0 / math.sqrt(2.0))))
    normal_pdf = jnp.exp(-0.5 * inputs * inputs) * (1.0 / math.sqrt(2.0 * math.pi))
    return normal_cdf + inputs * normal_pdf

def lon_table():
    lon_ids = jnp.arange(NLON, dtype=jnp.int32)
    mode_ids = jnp.arange(MODES, dtype=jnp.int32)
    phase_index = lon_ids[:, None] * mode_ids[None, :] % NLON
    angle_rad = phase_index.astype(jnp.float32) * (2.0 * math.pi / NLON)
    paired = jnp.stack([jnp.cos(angle_rad), -jnp.sin(angle_rad)], axis=-1).astype(jnp.bfloat16)
    return paired.astype(jnp.float32).reshape(NLON, 2 * MODES)

def analyze_lon(grid_field, table_flat):
    summed = jnp.einsum('jq,jrc->qrc', table_flat, grid_field.astype(jnp.float32))
    return (summed * (1.0 / math.sqrt(NLON))).reshape(MODES, 2, NLAT, C).astype(jnp.bfloat16)

def synthesize_lon(spectral, table_flat):
    stacked = spectral.astype(jnp.float32).reshape(2 * MODES, NLAT, C)
    return jnp.einsum('jq,qrc->jrc', table_flat, stacked) * (1.0 / math.sqrt(NLON))

def banded_filter(disco_filter, slot_pairs, slot_count):
    slot_total = BANDS * SLOT_MAX
    slot_ids = jnp.arange(slot_total, dtype=jnp.int32)
    band_ids = slot_ids // SLOT_MAX
    in_use = slot_ids % SLOT_MAX < jnp.repeat(slot_count, SLOT_MAX, total_repeat_length=slot_total)
    out_rows = band_ids * LAT_DEV + slot_pairs[:, 0]
    in_rows = band_ids * LAT_DEV + slot_pairs[:, 0] + slot_pairs[:, 1] - REACH
    inside = in_use & (in_rows >= 0) & (in_rows < NLAT)
    weights = jnp.where(inside[:, None, None], disco_filter.astype(jnp.float32), jnp.float32(0.0))
    safe_rows = jnp.clip(in_rows, 0, NLAT - 1).astype(jnp.int32)
    banded = jnp.zeros((2, NLAT, NLAT, MODES), jnp.float32)
    return banded.at[:, out_rows, safe_rows, :].add(jnp.transpose(weights, (1, 0, 2)))

def apply_filter(banded, spectral):
    source = spectral.astype(jnp.float32)
    real_src = source[:, 0]
    imag_src = source[:, 1]

    def mix_rows(matrix, field_part):
        return jnp.einsum('oik,kic->koc', matrix, field_part)
    real_out = mix_rows(banded[0], real_src) - mix_rows(banded[1], imag_src)
    imag_out = mix_rows(banded[0], imag_src) + mix_rows(banded[1], real_src)
    return jnp.stack([real_out, imag_out], axis=1).astype(jnp.bfloat16)

def apply_adjoint(banded, gradient):
    source = gradient.astype(jnp.float32)
    real_src = source[:, 0]
    imag_src = source[:, 1]

    def mix_back(matrix, field_part):
        return jnp.einsum('oik,koc->kic', matrix, field_part)
    real_out = mix_back(banded[0], real_src) + mix_back(banded[1], imag_src)
    imag_out = mix_back(banded[0], imag_src) - mix_back(banded[1], real_src)
    return jnp.stack([real_out, imag_out], axis=1).astype(jnp.bfloat16)

def reference(field_in, cotangent, mlp_in_weight, mlp_out_weight, legendre_analysis, legendre_synthesis, spectral_gain, disco_filter, slot_pairs, slot_count):
    table_flat = lon_table()
    analysis = legendre_analysis.astype(jnp.float32).reshape(MODES, DEG, NLAT)
    synthesis = legendre_synthesis.astype(jnp.float32).reshape(MODES, NLAT, DEG)
    gain_table = spectral_gain.astype(jnp.float32)
    banded = banded_filter(disco_filter, slot_pairs, slot_count)
    spectrum = analyze_lon(field_in, table_flat)
    mixed = apply_filter(banded, spectrum)
    coeffs = jnp.einsum('kla,krac->krlc', analysis, mixed.astype(jnp.float32))
    filtered = (coeffs * gain_table).astype(jnp.bfloat16)
    synthesized = jnp.einsum('kal,krlc->krac', synthesis, filtered.astype(jnp.float32)).astype(jnp.bfloat16)
    spatial = synthesize_lon(synthesized, table_flat)
    hidden_in = (field_in.astype(jnp.float32) + spatial).astype(jnp.bfloat16)
    hidden_rows = hidden_in.reshape(NLON * NLAT, C)
    pre_act = jnp.dot(hidden_rows, mlp_in_weight, preferred_element_type=jnp.float32)
    grad_rows = cotangent.reshape(NLON * NLAT, C)
    grad_act = jnp.dot(grad_rows, mlp_out_weight.T, preferred_element_type=jnp.float32)
    grad_pre = (grad_act * gelu_slope(pre_act)).astype(jnp.bfloat16)
    grad_hidden = (grad_rows.astype(jnp.float32) + jnp.dot(grad_pre, mlp_in_weight.T, preferred_element_type=jnp.float32)).astype(jnp.bfloat16)
    grad_grid = grad_hidden.reshape(NLON, NLAT, C)
    grad_spectrum = analyze_lon(grad_grid, table_flat)
    grad_coeffs = jnp.einsum('kal,krac->krlc', synthesis, grad_spectrum.astype(jnp.float32))
    grad_filtered = (grad_coeffs * gain_table).astype(jnp.bfloat16)
    grad_mixed = jnp.einsum('kla,krlc->krac', analysis, grad_filtered.astype(jnp.float32)).astype(jnp.bfloat16)
    grad_source = apply_adjoint(banded, grad_mixed)
    return (grad_grid.astype(jnp.float32) + synthesize_lon(grad_source, table_flat)).astype(jnp.bfloat16)
```

```python
import math

import jax
import jax.numpy as jnp
from jax import lax
from jax.sharding import PartitionSpec as P

NLON = 720
MODES = 256
REACH = 2


def gelu_slope(inputs):
    normal_cdf = 0.5 * (1.0 + jax.scipy.special.erf(inputs * (1.0 / math.sqrt(2.0))))
    normal_pdf = jnp.exp(-0.5 * inputs * inputs) * (1.0 / math.sqrt(2.0 * math.pi))
    return normal_cdf + inputs * normal_pdf


def lon_tables(lon_ids, mode_ids):
    phase_index = lon_ids[:, None] * mode_ids[None, :] % NLON
    angle_rad = phase_index.astype(jnp.float32) * (2.0 * math.pi / NLON)
    return jnp.stack([jnp.cos(angle_rad), -jnp.sin(angle_rad)], axis=-1).astype(jnp.bfloat16)


def to_spectrum(grid_block):
    half_modes = MODES // lax.axis_size("lon")
    mode_ids = lax.axis_index("lon") * half_modes + jnp.arange(half_modes, dtype=jnp.int32)
    tail_shape = grid_block.shape[1:]
    piece_block = lax.all_gather(grid_block, "lon", axis=0, tiled=True)
    lon_count = piece_block.shape[0]
    lon_ids = jnp.arange(lon_count, dtype=jnp.int32)
    table_flat = lon_tables(lon_ids, mode_ids).reshape(lon_count, 2 * half_modes)
    summed = lax.dot_general(
        table_flat, piece_block, (((0,), (0,)), ((), ())), preferred_element_type=jnp.float32
    )
    return (
        (summed * (1.0 / math.sqrt(NLON)))
        .reshape((half_modes, 2) + tail_shape)
        .astype(jnp.bfloat16)
    )


def to_grid(band_block):
    lon_local = NLON // lax.axis_size("lon")
    lon_ids = lax.axis_index("lon") * lon_local + jnp.arange(lon_local, dtype=jnp.int32)
    tail_shape = band_block.shape[2:]
    piece_block = lax.all_gather(band_block, "lon", axis=0, tiled=True)
    mode_count = piece_block.shape[0]
    mode_ids = jnp.arange(mode_count, dtype=jnp.int32)
    table_flat = lon_tables(lon_ids, mode_ids).reshape(lon_local, 2 * mode_count)
    stacked = piece_block.reshape((2 * mode_count,) + tail_shape)
    summed = lax.dot_general(
        table_flat, stacked, (((1,), (0,)), ((), ())), preferred_element_type=jnp.float32
    )
    return summed * (1.0 / math.sqrt(NLON))


def to_owners(band_block):
    return lax.all_to_all(band_block, ("lat", "chan"), split_axis=0, concat_axis=2, tiled=True)


def to_bands(owned_block):
    return lax.all_to_all(owned_block, ("lat", "chan"), split_axis=2, concat_axis=0, tiled=True)


def band_filter(disco_filter, slot_pairs, slot_count, band_rows):
    width = 2 * REACH + 1
    in_use = jnp.arange(disco_filter.shape[0], dtype=jnp.int32) < slot_count[0]
    cell_of = slot_pairs[:, 0] * width + slot_pairs[:, 1]
    cells = jnp.arange(band_rows * width, dtype=jnp.int32)
    chosen = ((cells[:, None] == cell_of[None, :]) & in_use[None, :]).astype(jnp.bfloat16)
    return jnp.einsum(
        "ts,spk->tpk", chosen, disco_filter, preferred_element_type=jnp.float32
    ).astype(jnp.bfloat16)


def filter_matrices(cells, rows):
    width = 2 * REACH + 1
    by_row = cells.reshape(rows, width, 2, cells.shape[2])
    total = 0.0
    for offset in range(width):
        shifted = jnp.eye(rows, k=offset - REACH, dtype=jnp.bfloat16)
        total = total + jnp.transpose(by_row[:, offset], (2, 1, 0))[:, :, :, None] * shifted
    real, imag = total[:, 0], total[:, 1]
    return jnp.concatenate(
        [jnp.concatenate([real, -imag], axis=2), jnp.concatenate([imag, real], axis=2)], axis=1
    )


def per_device(
    field_in,
    cotangent,
    mlp_in_weight,
    mlp_out_weight,
    legendre_analysis,
    legendre_synthesis,
    spectral_gain,
    disco_filter,
    slot_pairs,
    slot_count,
):
    analysis = legendre_analysis.reshape(legendre_analysis.shape[1:])
    synthesis = legendre_synthesis.reshape(legendre_synthesis.shape[1:])
    gain_table = spectral_gain.astype(jnp.float32)
    channels = field_in.shape[2]
    weight_in, weight_out = (
        lax.all_gather(mlp_in_weight, "chan", axis=0, tiled=True),
        lax.all_gather(mlp_out_weight, "chan", axis=0, tiled=True),
    )
    cells = band_filter(disco_filter, slot_pairs, slot_count, field_in.shape[1])
    modes_owned = analysis.shape[0]
    rows = analysis.shape[2]
    all_cells = lax.all_gather(cells, ("lat", "chan"), axis=0, tiled=True)
    own_cells = lax.dynamic_slice_in_dim(
        all_cells, lax.axis_index(("lat", "chan")) * modes_owned, modes_owned, 2
    )
    filters = filter_matrices(own_cells, rows)
    owned = to_owners(to_spectrum(field_in))
    mixed = (
        jnp.einsum(
            "kxy,kyc->kxc",
            filters,
            owned.reshape(modes_owned, 2 * rows, channels),
            preferred_element_type=jnp.float32,
        )
        .astype(jnp.bfloat16)
        .reshape(owned.shape)
    )
    coeffs = jnp.einsum("kla,krac->krlc", analysis, mixed, preferred_element_type=jnp.float32)
    filtered = (coeffs * gain_table).astype(jnp.bfloat16)
    synthesized = jnp.einsum(
        "kal,krlc->krac", synthesis, filtered, preferred_element_type=jnp.float32
    ).astype(jnp.bfloat16)
    spatial = to_grid(to_bands(synthesized))
    hidden_in = (field_in.astype(jnp.float32) + spatial).astype(jnp.bfloat16)
    hidden_rows = hidden_in.reshape(-1, channels)
    pre_act = jnp.dot(hidden_rows, weight_in, preferred_element_type=jnp.float32)
    grad_rows = cotangent.reshape(-1, channels)
    grad_act = lax.dot_general(
        grad_rows, weight_out, (((1,), (1,)), ((), ())), preferred_element_type=jnp.float32
    )
    grad_pre = (grad_act * gelu_slope(pre_act)).astype(jnp.bfloat16)
    back_rows = lax.dot_general(
        grad_pre, weight_in, (((1,), (1,)), ((), ())), preferred_element_type=jnp.float32
    )
    grad_hidden = (grad_rows.astype(jnp.float32) + back_rows).astype(jnp.bfloat16)
    grad_grid = grad_hidden.reshape(cotangent.shape)
    grad_owned = to_owners(to_spectrum(grad_grid))
    grad_coeffs = jnp.einsum(
        "kal,krac->krlc", synthesis, grad_owned, preferred_element_type=jnp.float32
    )
    grad_filtered = (grad_coeffs * gain_table).astype(jnp.bfloat16)
    grad_mixed = jnp.einsum(
        "kla,krlc->krac", analysis, grad_filtered, preferred_element_type=jnp.float32
    ).astype(jnp.bfloat16)
    grad_source = (
        jnp.einsum(
            "kxy,kxc->kyc",
            filters,
            grad_mixed.reshape(modes_owned, 2 * rows, channels),
            preferred_element_type=jnp.float32,
        )
        .astype(jnp.bfloat16)
        .reshape(grad_mixed.shape)
    )
    grad_spatial = to_grid(to_bands(grad_source))
    return (grad_grid.astype(jnp.float32) + grad_spatial).astype(jnp.bfloat16)


def solution(mesh):
    return jax.shard_map(
        per_device,
        mesh=mesh,
        in_specs=(
            P(("groups", "lon"), ("lat", "chan"), None),
            P(("groups", "lon"), ("lat", "chan"), None),
            P("chan", None),
            P("chan", None),
            P("lon", ("lat", "chan"), None, None),
            P("lon", ("lat", "chan"), None, None),
            P(),
            P(("lat", "chan"), None, "lon"),
            P(("lat", "chan"), None),
            P(("lat", "chan")),
        ),
        out_specs=P(("groups", "lon"), ("lat", "chan"), None),
        check_vma=False,
    )
```

```python
import functools
import math

import jax
import jax.numpy as jnp
import numpy as np
from jax import lax
from jax.experimental import pallas as pl
from jax.experimental.pallas import tpu as pltpu
from jax.sharding import PartitionSpec as P

NLON = 720
MODES = 256
REACH = 2


def gelu_slope(inputs):
    normal_cdf = 0.5 * (1.0 + jax.scipy.special.erf(inputs * (1.0 / math.sqrt(2.0))))
    normal_pdf = jnp.exp(-0.5 * inputs * inputs) * (1.0 / math.sqrt(2.0 * math.pi))
    return normal_cdf + inputs * normal_pdf


def lon_tables(lon_ids, mode_ids):
    phase_index = lon_ids[:, None] * mode_ids[None, :] % NLON
    angle_rad = phase_index.astype(jnp.float32) * (2.0 * math.pi / NLON)
    return jnp.stack([jnp.cos(angle_rad), -jnp.sin(angle_rad)], axis=-1).astype(jnp.bfloat16)


def to_spectrum(grid_block):
    half_modes = MODES // lax.axis_size("lon")
    mode_ids = lax.axis_index("lon") * half_modes + jnp.arange(half_modes, dtype=jnp.int32)
    tail_shape = grid_block.shape[1:]
    piece_block = lax.all_gather(grid_block, "lon", axis=0, tiled=True)
    lon_count = piece_block.shape[0]
    lon_ids = jnp.arange(lon_count, dtype=jnp.int32)
    table_flat = lon_tables(lon_ids, mode_ids).reshape(lon_count, 2 * half_modes)
    summed = lax.dot_general(
        table_flat, piece_block, (((0,), (0,)), ((), ())), preferred_element_type=jnp.float32
    )
    return (
        (summed * (1.0 / math.sqrt(NLON)))
        .reshape((half_modes, 2) + tail_shape)
        .astype(jnp.bfloat16)
    )


def to_grid(band_block):
    lon_local = NLON // lax.axis_size("lon")
    lon_ids = lax.axis_index("lon") * lon_local + jnp.arange(lon_local, dtype=jnp.int32)
    tail_shape = band_block.shape[2:]
    piece_block = lax.all_gather(band_block, "lon", axis=0, tiled=True)
    mode_count = piece_block.shape[0]
    mode_ids = jnp.arange(mode_count, dtype=jnp.int32)
    table_flat = lon_tables(lon_ids, mode_ids).reshape(lon_local, 2 * mode_count)
    stacked = piece_block.reshape((2 * mode_count,) + tail_shape)
    summed = lax.dot_general(
        table_flat, stacked, (((1,), (0,)), ((), ())), preferred_element_type=jnp.float32
    )
    return summed * (1.0 / math.sqrt(NLON))


def to_owners(band_block):
    return lax.all_to_all(band_block, ("lat", "chan"), split_axis=0, concat_axis=2, tiled=True)


def to_bands(owned_block):
    return lax.all_to_all(owned_block, ("lat", "chan"), split_axis=2, concat_axis=0, tiled=True)


def band_filter(disco_filter, slot_pairs, slot_count, band_rows):
    width = 2 * REACH + 1
    in_use = jnp.arange(disco_filter.shape[0], dtype=jnp.int32) < slot_count[0]
    cell_of = slot_pairs[:, 0] * width + slot_pairs[:, 1]
    cells = jnp.arange(band_rows * width, dtype=jnp.int32)
    chosen = ((cells[:, None] == cell_of[None, :]) & in_use[None, :]).astype(jnp.bfloat16)
    return jnp.einsum(
        "ts,spk->tpk", chosen, disco_filter, preferred_element_type=jnp.float32
    ).astype(jnp.bfloat16)


def filter_matrices(cells, rows):
    width = 2 * REACH + 1
    by_row = cells.reshape(rows, width, 2, cells.shape[2])
    total = 0.0
    for offset in range(width):
        shifted = jnp.eye(rows, k=offset - REACH, dtype=jnp.bfloat16)
        total = total + jnp.transpose(by_row[:, offset], (2, 1, 0))[:, :, :, None] * shifted
    real, imag = total[:, 0], total[:, 1]
    return jnp.concatenate(
        [jnp.concatenate([real, -imag], axis=2), jnp.concatenate([imag, real], axis=2)], axis=1
    )


def per_device_plain(
    field_in,
    cotangent,
    mlp_in_weight,
    mlp_out_weight,
    legendre_analysis,
    legendre_synthesis,
    spectral_gain,
    disco_filter,
    slot_pairs,
    slot_count,
):
    analysis = legendre_analysis.reshape(legendre_analysis.shape[1:])
    synthesis = legendre_synthesis.reshape(legendre_synthesis.shape[1:])
    gain_table = spectral_gain.astype(jnp.float32)
    channels = field_in.shape[2]
    weight_in, weight_out = (
        lax.all_gather(mlp_in_weight, "chan", axis=0, tiled=True),
        lax.all_gather(mlp_out_weight, "chan", axis=0, tiled=True),
    )
    cells = band_filter(disco_filter, slot_pairs, slot_count, field_in.shape[1])
    modes_owned = analysis.shape[0]
    rows = analysis.shape[2]
    all_cells = lax.all_gather(cells, ("lat", "chan"), axis=0, tiled=True)
    own_cells = lax.dynamic_slice_in_dim(
        all_cells, lax.axis_index(("lat", "chan")) * modes_owned, modes_owned, 2
    )
    filters = filter_matrices(own_cells, rows)
    owned = to_owners(to_spectrum(field_in))
    mixed = (
        jnp.einsum(
            "kxy,kyc->kxc",
            filters,
            owned.reshape(modes_owned, 2 * rows, channels),
            preferred_element_type=jnp.float32,
        )
        .astype(jnp.bfloat16)
        .reshape(owned.shape)
    )
    coeffs = jnp.einsum("kla,krac->krlc", analysis, mixed, preferred_element_type=jnp.float32)
    filtered = (coeffs * gain_table).astype(jnp.bfloat16)
    synthesized = jnp.einsum(
        "kal,krlc->krac", synthesis, filtered, preferred_element_type=jnp.float32
    ).astype(jnp.bfloat16)
    spatial = to_grid(to_bands(synthesized))
    hidden_in = (field_in.astype(jnp.float32) + spatial).astype(jnp.bfloat16)
    hidden_rows = hidden_in.reshape(-1, channels)
    pre_act = jnp.dot(hidden_rows, weight_in, preferred_element_type=jnp.float32)
    grad_rows = cotangent.reshape(-1, channels)
    grad_act = lax.dot_general(
        grad_rows, weight_out, (((1,), (1,)), ((), ())), preferred_element_type=jnp.float32
    )
    grad_pre = (grad_act * gelu_slope(pre_act)).astype(jnp.bfloat16)
    back_rows = lax.dot_general(
        grad_pre, weight_in, (((1,), (1,)), ((), ())), preferred_element_type=jnp.float32
    )
    grad_hidden = (grad_rows.astype(jnp.float32) + back_rows).astype(jnp.bfloat16)
    grad_grid = grad_hidden.reshape(cotangent.shape)
    grad_owned = to_owners(to_spectrum(grad_grid))
    grad_coeffs = jnp.einsum(
        "kal,krac->krlc", synthesis, grad_owned, preferred_element_type=jnp.float32
    )
    grad_filtered = (grad_coeffs * gain_table).astype(jnp.bfloat16)
    grad_mixed = jnp.einsum(
        "kla,krlc->krac", analysis, grad_filtered, preferred_element_type=jnp.float32
    ).astype(jnp.bfloat16)
    grad_source = (
        jnp.einsum(
            "kxy,kxc->kyc",
            filters,
            grad_mixed.reshape(modes_owned, 2 * rows, channels),
            preferred_element_type=jnp.float32,
        )
        .astype(jnp.bfloat16)
        .reshape(grad_mixed.shape)
    )
    grad_spatial = to_grid(to_bands(grad_source))
    return (grad_grid.astype(jnp.float32) + grad_spatial).astype(jnp.bfloat16)


def fixed_tables(bands, modes, lon_pad):
    halves = MODES // (bands * modes)
    lon_ids = np.arange(NLON, dtype=np.int32)
    mode_ids = np.arange(MODES, dtype=np.int32)
    phase_index = lon_ids[:, None] * mode_ids[None, :] % NLON
    angle_rad = phase_index.astype(np.float32) * np.float32(2.0 * math.pi / NLON)
    paired = np.stack([np.cos(angle_rad), -np.sin(angle_rad)], axis=0)
    blocks = paired.reshape(2, halves, NLON // halves, halves, bands, modes)
    blocks = blocks.transpose(3, 1, 4, 0, 5, 2).reshape(halves, halves, bands * 2 * modes, -1)
    blocks = np.pad(blocks, ((0, 0), (0, 0), (0, 0), (0, lon_pad - blocks.shape[3])))
    return blocks.astype(jnp.bfloat16)


def block_kernel(
    sizes,
    field,
    cot,
    win_own,
    wout_own,
    pieces,
    left,
    right,
    left_t,
    right_t,
    gain,
    table_in,
    table_out,
    out,
    other,
    sent,
    landed,
    back_sent,
    back_landed,
    back_other,
    pieces_all,
    pieces_f32,
    strided_in,
    strided_out,
    win,
    wout,
    grad_act,
    hidden,
    lon_sem,
    go_sem,
    back_sem,
    swap_sem,
    piece_sem,
    weight_sem,
):
    bands, chans, rows, modes, channels, chunks = sizes
    width = 2 * rows * modes
    per_row = 2 * modes
    total = bands * width
    lat, chan, lon = lax.axis_index("lat"), lax.axis_index("chan"), lax.axis_index("lon")
    me = lat * chans + chan
    mate = {"lon": 1 - lon}
    scale = 1.0 / math.sqrt(NLON)
    started = []

    def band_at(step):
        band = lax.rem(me + step, bands)
        return band, {"lat": band // chans, "chan": lax.rem(band, chans)}

    def send(src, dst, sems, where):
        copy = pltpu.make_async_remote_copy(
            src_ref=src,
            dst_ref=dst,
            send_sem=sems.at[0],
            recv_sem=sems.at[1],
            device_id=where,
            device_id_type=pl.DeviceIdType.MESH,
        )
        copy.start()
        started.append(copy)
        return copy

    barrier = pltpu.get_barrier_semaphore()
    for step in range(1, bands):
        pl.semaphore_signal(
            barrier, inc=1, device_id=band_at(step)[1], device_id_type=pl.DeviceIdType.MESH
        )
    pl.semaphore_signal(barrier, inc=1, device_id=mate, device_id_type=pl.DeviceIdType.MESH)
    pl.semaphore_wait(barrier, bands)

    def swap_lon(source, leg):
        return [
            send(source.at[:, :, cs], other.at[leg, :, :, cs], lon_sem.at[leg, c], mate)
            for c, cs in enumerate(chunks)
        ]

    def to_owner(source, leg, c, copy):
        cs = chunks[c]
        copy.wait_recv()

        @pl.loop(0, rows)
        def _(row):
            summed = jnp.dot(
                table_in[lon], source[row, :, cs], preferred_element_type=jnp.float32
            ) + jnp.dot(
                table_in[1 - lon], other[leg, row, :, cs], preferred_element_type=jnp.float32
            )
            at = pl.ds(pl.multiple_of(row * per_row, per_row), per_row)
            sent[leg, :, at, cs] = (
                (summed * scale).astype(jnp.bfloat16).reshape(bands, per_row, -1)
            )

        copies = []
        for step in range(1, bands):
            band, where = band_at(step)
            copies.append(
                send(
                    sent.at[leg, band, :, cs],
                    landed.at[leg, me, :, cs],
                    go_sem.at[leg, c, step - 1],
                    where,
                )
            )
        landed[leg, me, :, cs] = sent[leg, me, :, cs]
        return copies

    def spectral(leg, c, copies):
        cs = chunks[c]
        tiles = cs.size // 128
        for copy in copies:
            copy.wait_recv()
        for tile in range(tiles):
            lanes = pl.ds(cs.start + tile * 128, 128)
            strided_in[pl.ds(tile * total, total), :] = (
                landed[leg, :, :, lanes].reshape(total, 128).astype(jnp.float32)
            )

        @pl.loop(0, modes)
        def _(mode):
            at = [pl.ds(tile * total + mode, 2 * rows * bands, stride=modes) for tile in range(tiles)]
            source = jnp.concatenate([strided_in[a, :] for a in at], axis=1).astype(jnp.bfloat16)
            eight = pl.ds(pl.multiple_of(mode * 8, 8), 8)
            filt = pieces_f32[:, eight, :].reshape(bands * 8, pieces_f32.shape[2])
            filt = filt[:, : 2 * rows * bands].astype(jnp.bfloat16)
            if leg == 0:
                source = jnp.dot(filt, source, preferred_element_type=jnp.float32)
                source = source.astype(jnp.bfloat16)
                first, second = left, right
            else:
                first, second = right_t, left_t
            coeffs = jnp.dot(first[mode], source, preferred_element_type=jnp.float32)
            degrees = coeffs.shape[0] // 2
            gained = (coeffs.reshape(2, degrees, -1) * gain[:, cs][None]).astype(jnp.bfloat16)
            result = jnp.dot(
                second[mode],
                gained.reshape(2 * degrees, -1),
                preferred_element_type=jnp.float32,
            )
            if leg == 1:
                result = lax.dot_general(
                    filt,
                    result.astype(jnp.bfloat16),
                    (((0,), (0,)), ((), ())),
                    preferred_element_type=jnp.float32,
                )
            for tile in range(tiles):
                strided_out[at[tile], :] = result[:, tile * 128 : (tile + 1) * 128]

        for tile in range(tiles):
            lanes = pl.ds(cs.start + tile * 128, 128)
            back_sent[leg, :, :, lanes] = (
                strided_out[pl.ds(tile * total, total), :]
                .astype(jnp.bfloat16)
                .reshape(bands, width, 128)
            )
        back = []
        for step in range(1, bands):
            band, where = band_at(step)
            back.append(
                send(
                    back_sent.at[leg, band, :, cs],
                    back_landed.at[leg, me, :, cs],
                    back_sem.at[leg, c, step - 1],
                    where,
                )
            )
        back_landed[leg, me, :, cs] = back_sent[leg, me, :, cs]
        return back

    def swap_back(leg, c, copies):
        cs = chunks[c]
        for copy in copies:
            copy.wait_recv()
        return send(
            back_landed.at[leg, :, :, cs], back_other.at[leg, :, :, cs], swap_sem.at[leg, c], mate
        )

    def to_grid_rows(base, target, leg, c, copy):
        cs = chunks[c]
        copy.wait_recv()

        @pl.loop(0, rows)
        def _(row):
            at = pl.ds(pl.multiple_of(row * per_row, per_row), per_row)
            near = back_landed[leg, :, at, cs].reshape(bands * per_row, -1)
            far = back_other[leg, :, at, cs].reshape(bands * per_row, -1)
            summed = jnp.dot(
                table_out[lon], near, preferred_element_type=jnp.float32
            ) + jnp.dot(table_out[1 - lon], far, preferred_element_type=jnp.float32)
            target[row, :, cs] = (base[row, :, cs].astype(jnp.float32) + summed * scale).astype(
                jnp.bfloat16
            )

    count = range(len(chunks))
    first_swap = swap_lon(field, 0)
    piece_copies = []
    for step in range(1, bands):
        band, where = band_at(step)
        piece_copies.append(
            send(pieces.at[band], pieces_all.at[me], piece_sem.at[step - 1], where)
        )
    pieces_all[me] = pieces[me]
    going = [to_owner(field, 0, c, first_swap[c]) for c in count]

    held = win_own.shape[0]
    mine = pl.ds(pl.multiple_of(chan * held, 16), held)
    beside = {"chan": 1 - chan}
    weight_copies = [
        send(wout_own, wout.at[mine], weight_sem.at[0], beside),
        send(win_own, win.at[mine], weight_sem.at[1], beside),
    ]
    win[mine, :] = win_own[...]
    wout[mine, :] = wout_own[...]

    for copy in piece_copies:
        copy.wait_recv()
    pieces_f32[...] = pieces_all[...].astype(jnp.float32)
    coming = [spectral(0, c, going[c]) for c in count]
    for copy in weight_copies:
        copy.wait_recv()

    @pl.loop(0, rows)
    def _(row):
        grad_act[row] = lax.dot_general(
            cot[row], wout[...], (((1,), (1,)), ((), ())), preferred_element_type=jnp.float32
        )

    swapped = [swap_back(0, c, coming[c]) for c in count]
    for c in count:
        to_grid_rows(field, hidden, 0, c, swapped[c])

    @pl.loop(0, rows)
    def _(row):
        pre_act = jnp.dot(hidden[row], win[...], preferred_element_type=jnp.float32)
        grad_pre = (grad_act[row] * gelu_slope(pre_act)).astype(jnp.bfloat16)
        back_rows = lax.dot_general(
            grad_pre, win[...], (((1,), (1,)), ((), ())), preferred_element_type=jnp.float32
        )
        hidden[row] = (cot[row].astype(jnp.float32) + back_rows).astype(jnp.bfloat16)

    second_swap = swap_lon(hidden, 1)
    going = [to_owner(hidden, 1, c, second_swap[c]) for c in count]
    coming = [spectral(1, c, going[c]) for c in count]
    swapped = [swap_back(1, c, coming[c]) for c in count]
    for c in count:
        to_grid_rows(hidden, out, 1, c, swapped[c])
    for copy in started:
        copy.wait_send()


def per_device(
    field_in,
    cotangent,
    mlp_in_weight,
    mlp_out_weight,
    legendre_analysis,
    legendre_synthesis,
    spectral_gain,
    disco_filter,
    slot_pairs,
    slot_count,
):
    chans = lax.axis_size("chan")
    bands = lax.axis_size("lat") * chans
    lon_local, rows, channels = field_in.shape
    _, modes, degrees, all_rows = legendre_analysis.shape
    lon = lax.axis_index("lon")
    band = lax.axis_index(("lat", "chan"))
    lon_pad = -(-lon_local // 16) * 16

    def rows_first(grid_block):
        return jnp.pad(
            jnp.transpose(grid_block, (1, 0, 2)), ((0, 0), (0, lon_pad - lon_local), (0, 0))
        )

    cells = band_filter(disco_filter, slot_pairs, slot_count, rows)
    span = 2 * REACH + 1
    by_row = cells.reshape(rows, span, 2, bands, modes)
    places = band * rows - REACH + jnp.arange(rows)[:, None] + jnp.arange(span)[None, :]
    hits = (places[:, :, None] == jnp.arange(all_rows)).astype(jnp.bfloat16)
    spread = jnp.einsum(
        "rqpbm,rqi->pbmri", by_row, hits, preferred_element_type=jnp.float32
    ).astype(jnp.bfloat16)
    real, imag = spread[0], spread[1]
    pieces = jnp.stack(
        [jnp.stack([real, -imag], axis=-1), jnp.stack([imag, real], axis=-1)], axis=2
    ).reshape(bands, modes, 2 * rows, 2 * all_rows)
    lanes = -(-2 * all_rows // 128) * 128
    pieces = jnp.pad(
        pieces, ((0, 0), (0, 0), (0, 8 - 2 * rows), (0, lanes - 2 * all_rows))
    ).reshape(bands, modes * 8, lanes)

    both = jnp.eye(2, dtype=jnp.bfloat16)
    analysis = legendre_analysis[0].reshape(modes, degrees, bands, rows)
    synthesis = legendre_synthesis[0]
    left = (analysis[:, None, :, :, None, :] * both[None, :, None, None, :, None]).reshape(
        modes, 2, degrees, bands, 2 * rows
    )
    left = jnp.pad(left, ((0, 0),) * 4 + ((0, 8 - 2 * rows),)).reshape(
        modes, 2 * degrees, bands * 8
    )
    right = (synthesis[:, :, None, None, :] * both[None, None, :, :, None]).reshape(
        modes, 2 * all_rows, 2 * degrees
    )
    left_t = jnp.swapaxes(left, 1, 2)
    right_t = jnp.swapaxes(right, 1, 2)
    table = fixed_tables(bands, modes, lon_pad)
    table_in = lax.dynamic_index_in_dim(jnp.asarray(table), lon, 0, keepdims=False)
    table_out = lax.dynamic_index_in_dim(
        jnp.asarray(table.transpose(1, 0, 3, 2)), lon, 0, keepdims=False
    )

    chunks = tuple(pl.ds(start, size) for start, size in split_channels(channels))
    width = 2 * rows * modes
    widest = max(chunk.size for chunk in chunks) // 128
    held = (2, bands, width, channels)
    grid_shape = (rows, lon_pad, channels)
    bf16, f32 = jnp.bfloat16, jnp.float32
    vmem = pl.BlockSpec(memory_space=pltpu.VMEM)
    dma = pltpu.SemaphoreType.DMA
    result = pl.pallas_call(
        functools.partial(block_kernel, (bands, chans, rows, modes, channels, chunks)),
        out_shape=jax.ShapeDtypeStruct(grid_shape, bf16),
        in_specs=[vmem] * 12,
        out_specs=vmem,
        scratch_shapes=[
            pltpu.VMEM((2,) + grid_shape, bf16),
            pltpu.VMEM(held, bf16),
            pltpu.VMEM(held, bf16),
            pltpu.VMEM(held, bf16),
            pltpu.VMEM(held, bf16),
            pltpu.VMEM(held, bf16),
            pltpu.VMEM(pieces.shape, bf16),
            pltpu.VMEM(pieces.shape, f32),
            pltpu.VMEM((widest * bands * width, 128), f32),
            pltpu.VMEM((widest * bands * width, 128), f32),
            pltpu.VMEM((channels, mlp_in_weight.shape[1]), bf16),
            pltpu.VMEM((mlp_out_weight.shape[0] * chans, channels), bf16),
            pltpu.VMEM((rows, lon_pad, mlp_in_weight.shape[1]), f32),
            pltpu.VMEM(grid_shape, bf16),
            dma((2, len(chunks), 2)),
            dma((2, len(chunks), bands - 1, 2)),
            dma((2, len(chunks), bands - 1, 2)),
            dma((2, len(chunks), 2)),
            dma((bands - 1, 2)),
            dma((2, 2)),
        ],
        compiler_params=pltpu.CompilerParams(
            collective_id=0, has_side_effects=True, vmem_limit_bytes=56 * 1024 * 1024
        ),
    )(
        rows_first(field_in),
        rows_first(cotangent),
        mlp_in_weight,
        mlp_out_weight,
        pieces,
        left,
        right,
        left_t,
        right_t,
        spectral_gain.astype(f32),
        table_in,
        table_out,
    )
    return jnp.transpose(result[:, :lon_local], (1, 0, 2))


def split_channels(channels):
    tiles = channels // 128
    head = 128 * (tiles // 4 * 2 + tiles % 2)
    return [(0, channels - head), (channels - head, head)] if 0 < head < channels else [(0, channels)]


def solution(mesh):
    owned = MODES // (mesh.shape["lon"] * mesh.shape["lat"] * mesh.shape["chan"])
    fused = owned % 16 == 0 and mesh.shape["chan"] == 2 and mesh.shape["lon"] == 2
    return jax.shard_map(
        per_device if fused else per_device_plain,
        mesh=mesh,
        in_specs=(
            P(("groups", "lon"), ("lat", "chan"), None),
            P(("groups", "lon"), ("lat", "chan"), None),
            P("chan", None),
            P("chan", None),
            P("lon", ("lat", "chan"), None, None),
            P("lon", ("lat", "chan"), None, None),
            P(),
            P(("lat", "chan"), None, "lon"),
            P(("lat", "chan"), None),
            P(("lat", "chan")),
        ),
        out_specs=P(("groups", "lon"), ("lat", "chan"), None),
        check_vma=False,
    )
```

```python
import functools
import math

import jax
import jax.numpy as jnp
import numpy as np
from jax import lax
from jax.experimental import pallas as pl
from jax.experimental.pallas import tpu as pltpu
from jax.sharding import PartitionSpec as P

NLON = 720
MODES = 256
REACH = 2


def gelu_slope(inputs):
    normal_cdf = 0.5 * (1.0 + jax.scipy.special.erf(inputs * (1.0 / math.sqrt(2.0))))
    normal_pdf = jnp.exp(-0.5 * inputs * inputs) * (1.0 / math.sqrt(2.0 * math.pi))
    return normal_cdf + inputs * normal_pdf


def lon_tables(lon_ids, mode_ids):
    phase_index = lon_ids[:, None] * mode_ids[None, :] % NLON
    angle_rad = phase_index.astype(jnp.float32) * (2.0 * math.pi / NLON)
    return jnp.stack([jnp.cos(angle_rad), -jnp.sin(angle_rad)], axis=-1).astype(jnp.bfloat16)


def to_spectrum(grid_block):
    half_modes = MODES // lax.axis_size("lon")
    mode_ids = lax.axis_index("lon") * half_modes + jnp.arange(half_modes, dtype=jnp.int32)
    tail_shape = grid_block.shape[1:]
    piece_block = lax.all_gather(grid_block, "lon", axis=0, tiled=True)
    lon_count = piece_block.shape[0]
    lon_ids = jnp.arange(lon_count, dtype=jnp.int32)
    table_flat = lon_tables(lon_ids, mode_ids).reshape(lon_count, 2 * half_modes)
    summed = lax.dot_general(
        table_flat, piece_block, (((0,), (0,)), ((), ())), preferred_element_type=jnp.float32
    )
    return (
        (summed * (1.0 / math.sqrt(NLON)))
        .reshape((half_modes, 2) + tail_shape)
        .astype(jnp.bfloat16)
    )


def to_grid(band_block):
    lon_local = NLON // lax.axis_size("lon")
    lon_ids = lax.axis_index("lon") * lon_local + jnp.arange(lon_local, dtype=jnp.int32)
    tail_shape = band_block.shape[2:]
    piece_block = lax.all_gather(band_block, "lon", axis=0, tiled=True)
    mode_count = piece_block.shape[0]
    mode_ids = jnp.arange(mode_count, dtype=jnp.int32)
    table_flat = lon_tables(lon_ids, mode_ids).reshape(lon_local, 2 * mode_count)
    stacked = piece_block.reshape((2 * mode_count,) + tail_shape)
    summed = lax.dot_general(
        table_flat, stacked, (((1,), (0,)), ((), ())), preferred_element_type=jnp.float32
    )
    return summed * (1.0 / math.sqrt(NLON))


def to_owners(band_block):
    return lax.all_to_all(band_block, ("lat", "chan"), split_axis=0, concat_axis=2, tiled=True)


def to_bands(owned_block):
    return lax.all_to_all(owned_block, ("lat", "chan"), split_axis=2, concat_axis=0, tiled=True)


def band_filter(disco_filter, slot_pairs, slot_count, band_rows):
    width = 2 * REACH + 1
    in_use = jnp.arange(disco_filter.shape[0], dtype=jnp.int32) < slot_count[0]
    cell_of = slot_pairs[:, 0] * width + slot_pairs[:, 1]
    cells = jnp.arange(band_rows * width, dtype=jnp.int32)
    chosen = ((cells[:, None] == cell_of[None, :]) & in_use[None, :]).astype(jnp.bfloat16)
    return jnp.einsum(
        "ts,spk->tpk", chosen, disco_filter, preferred_element_type=jnp.float32
    ).astype(jnp.bfloat16)


def filter_matrices(cells, rows):
    width = 2 * REACH + 1
    by_row = cells.reshape(rows, width, 2, cells.shape[2])
    total = 0.0
    for offset in range(width):
        shifted = jnp.eye(rows, k=offset - REACH, dtype=jnp.bfloat16)
        total = total + jnp.transpose(by_row[:, offset], (2, 1, 0))[:, :, :, None] * shifted
    real, imag = total[:, 0], total[:, 1]
    return jnp.concatenate(
        [jnp.concatenate([real, -imag], axis=2), jnp.concatenate([imag, real], axis=2)], axis=1
    )


def per_device_plain(
    field_in,
    cotangent,
    mlp_in_weight,
    mlp_out_weight,
    legendre_analysis,
    legendre_synthesis,
    spectral_gain,
    disco_filter,
    slot_pairs,
    slot_count,
):
    analysis = legendre_analysis.reshape(legendre_analysis.shape[1:])
    synthesis = legendre_synthesis.reshape(legendre_synthesis.shape[1:])
    gain_table = spectral_gain.astype(jnp.float32)
    channels = field_in.shape[2]
    weight_in, weight_out = (
        lax.all_gather(mlp_in_weight, "chan", axis=0, tiled=True),
        lax.all_gather(mlp_out_weight, "chan", axis=0, tiled=True),
    )
    cells = band_filter(disco_filter, slot_pairs, slot_count, field_in.shape[1])
    modes_owned = analysis.shape[0]
    rows = analysis.shape[2]
    all_cells = lax.all_gather(cells, ("lat", "chan"), axis=0, tiled=True)
    own_cells = lax.dynamic_slice_in_dim(
        all_cells, lax.axis_index(("lat", "chan")) * modes_owned, modes_owned, 2
    )
    filters = filter_matrices(own_cells, rows)
    owned = to_owners(to_spectrum(field_in))
    mixed = (
        jnp.einsum(
            "kxy,kyc->kxc",
            filters,
            owned.reshape(modes_owned, 2 * rows, channels),
            preferred_element_type=jnp.float32,
        )
        .astype(jnp.bfloat16)
        .reshape(owned.shape)
    )
    coeffs = jnp.einsum("kla,krac->krlc", analysis, mixed, preferred_element_type=jnp.float32)
    filtered = (coeffs * gain_table).astype(jnp.bfloat16)
    synthesized = jnp.einsum(
        "kal,krlc->krac", synthesis, filtered, preferred_element_type=jnp.float32
    ).astype(jnp.bfloat16)
    spatial = to_grid(to_bands(synthesized))
    hidden_in = (field_in.astype(jnp.float32) + spatial).astype(jnp.bfloat16)
    hidden_rows = hidden_in.reshape(-1, channels)
    pre_act = jnp.dot(hidden_rows, weight_in, preferred_element_type=jnp.float32)
    grad_rows = cotangent.reshape(-1, channels)
    grad_act = lax.dot_general(
        grad_rows, weight_out, (((1,), (1,)), ((), ())), preferred_element_type=jnp.float32
    )
    grad_pre = (grad_act * gelu_slope(pre_act)).astype(jnp.bfloat16)
    back_rows = lax.dot_general(
        grad_pre, weight_in, (((1,), (1,)), ((), ())), preferred_element_type=jnp.float32
    )
    grad_hidden = (grad_rows.astype(jnp.float32) + back_rows).astype(jnp.bfloat16)
    grad_grid = grad_hidden.reshape(cotangent.shape)
    grad_owned = to_owners(to_spectrum(grad_grid))
    grad_coeffs = jnp.einsum(
        "kal,krac->krlc", synthesis, grad_owned, preferred_element_type=jnp.float32
    )
    grad_filtered = (grad_coeffs * gain_table).astype(jnp.bfloat16)
    grad_mixed = jnp.einsum(
        "kla,krlc->krac", analysis, grad_filtered, preferred_element_type=jnp.float32
    ).astype(jnp.bfloat16)
    grad_source = (
        jnp.einsum(
            "kxy,kxc->kyc",
            filters,
            grad_mixed.reshape(modes_owned, 2 * rows, channels),
            preferred_element_type=jnp.float32,
        )
        .astype(jnp.bfloat16)
        .reshape(grad_mixed.shape)
    )
    grad_spatial = to_grid(to_bands(grad_source))
    return (grad_grid.astype(jnp.float32) + grad_spatial).astype(jnp.bfloat16)


def fixed_tables(bands, modes, lon_pad):
    halves = MODES // (bands * modes)
    lon_ids = np.arange(NLON, dtype=np.int32)
    mode_ids = np.arange(MODES, dtype=np.int32)
    phase_index = lon_ids[:, None] * mode_ids[None, :] % NLON
    angle_rad = phase_index.astype(np.float32) * np.float32(2.0 * math.pi / NLON)
    paired = np.stack([np.cos(angle_rad), -np.sin(angle_rad)], axis=0)
    blocks = paired.reshape(2, halves, NLON // halves, halves, bands, modes)
    blocks = blocks.transpose(3, 1, 4, 0, 5, 2).reshape(halves, halves, bands * 2 * modes, -1)
    blocks = np.pad(blocks, ((0, 0), (0, 0), (0, 0), (0, lon_pad - blocks.shape[3])))
    return blocks.astype(jnp.bfloat16)


def block_kernel(
    sizes,
    field,
    cot,
    win_own,
    wout_own,
    disco,
    cell_places,
    analysis,
    synthesis,
    to_eights,
    to_pairs,
    gain_in,
    table_in,
    table_out,
    out,
    field_pad,
    gain,
    left,
    right,
    left_t,
    right_t,
    pieces,
    pre_act,
    grad_pre,
    other,
    sent,
    landed,
    back_sent,
    back_landed,
    back_other,
    pieces_all,
    pieces_f32,
    strided_in,
    strided_out,
    win,
    wout,
    grad_act,
    hidden,
    lon_sem,
    go_sem,
    back_sem,
    swap_sem,
    piece_sem,
    weight_sem,
):
    bands, chans, rows, modes, channels, chunks = sizes
    width = 2 * rows * modes
    per_row = 2 * modes
    total = bands * width
    lat, chan, lon = lax.axis_index("lat"), lax.axis_index("chan"), lax.axis_index("lon")
    me = lat * chans + chan
    mate = {"lon": 1 - lon}
    lons = field.shape[1]
    scale = 1.0 / math.sqrt(NLON)
    started = []

    def band_at(step):
        band = lax.rem(me + step, bands)
        return band, {"lat": band // chans, "chan": lax.rem(band, chans)}

    def send(src, dst, sems, where):
        copy = pltpu.make_async_remote_copy(
            src_ref=src,
            dst_ref=dst,
            send_sem=sems.at[0],
            recv_sem=sems.at[1],
            device_id=where,
            device_id_type=pl.DeviceIdType.MESH,
        )
        copy.start()
        started.append(copy)
        return copy

    barrier = pltpu.get_barrier_semaphore()
    for step in range(1, bands):
        pl.semaphore_signal(
            barrier, inc=1, device_id=band_at(step)[1], device_id_type=pl.DeviceIdType.MESH
        )
    pl.semaphore_signal(barrier, inc=1, device_id=mate, device_id_type=pl.DeviceIdType.MESH)
    pl.semaphore_wait(barrier, bands)

    def swap_lon(source, leg, c):
        cs = chunks[c]
        return send(source.at[:, :, cs], other.at[leg, :, :, cs], lon_sem.at[leg, c], mate)

    def stack_parts(wide, tall, wide_ref, tall_ref, wide_places, tall_places):
        @pl.loop(0, modes, unroll=4)
        def _(mode):
            degrees = wide.shape[2]
            for part in range(2):
                wide_ref[mode, part] = jnp.dot(
                    wide_places[part], wide[mode], preferred_element_type=jnp.float32
                ).astype(jnp.bfloat16)
                tall_ref[mode, part * degrees : (part + 1) * degrees, :] = lax.dot_general(
                    tall[mode],
                    tall_places[part],
                    (((0,), (1,)), ((), ())),
                    preferred_element_type=jnp.float32,
                ).astype(jnp.bfloat16)

    def to_owner(source, leg, c, copy):
        cs = chunks[c]
        copy.wait_recv()

        @pl.loop(0, rows)
        def _(row):
            summed = jnp.dot(
                table_in[lon, lon], source[row, :, cs], preferred_element_type=jnp.float32
            ) + jnp.dot(
                table_in[lon, 1 - lon], other[leg, row, :, cs], preferred_element_type=jnp.float32
            )
            at = pl.ds(pl.multiple_of(row * per_row, per_row), per_row)
            sent[leg, :, at, cs] = (
                (summed * scale).astype(jnp.bfloat16).reshape(bands, per_row, -1)
            )

        copies = []
        for step in range(1, bands):
            band, where = band_at(step)
            copies.append(
                send(
                    sent.at[leg, band, :, cs],
                    landed.at[leg, me, :, cs],
                    go_sem.at[leg, c, step - 1],
                    where,
                )
            )
        landed[leg, me, :, cs] = sent[leg, me, :, cs]
        return copies

    def spectral(leg, c, copies):
        cs = chunks[c]
        tiles = cs.size // 128
        for copy in copies:
            copy.wait_recv()
        for tile in range(tiles):
            lanes = pl.ds(cs.start + tile * 128, 128)
            strided_in[pl.ds(tile * total, total), :] = (
                landed[leg, :, :, lanes].reshape(total, 128).astype(jnp.float32)
            )

        @pl.loop(0, modes, unroll=4)
        def _(mode):
            at = [pl.ds(tile * total + mode, 2 * rows * bands, stride=modes) for tile in range(tiles)]
            source = jnp.concatenate([strided_in[a, :] for a in at], axis=1).astype(jnp.bfloat16)
            eight = pl.ds(pl.multiple_of(mode * 8, 8), 8)
            filt = pieces_f32[:, eight, :].reshape(bands * 8, pieces_f32.shape[2])
            filt = filt[:, : 2 * rows * bands].astype(jnp.bfloat16)
            if leg == 0:
                source = jnp.dot(filt, source, preferred_element_type=jnp.float32)
                source = source.astype(jnp.bfloat16)
                first, second = left, right
            else:
                first, second = right_t, left_t
            coeffs = jnp.dot(first[mode], source, preferred_element_type=jnp.float32)
            degrees = coeffs.shape[0] // 2
            gained = (coeffs.reshape(2, degrees, -1) * gain[:, cs][None]).astype(jnp.bfloat16)
            result = jnp.dot(
                second[mode, 0], gained[0], preferred_element_type=jnp.float32
            ) + jnp.dot(second[mode, 1], gained[1], preferred_element_type=jnp.float32)
            if leg == 1:
                result = lax.dot_general(
                    filt,
                    result.astype(jnp.bfloat16),
                    (((0,), (0,)), ((), ())),
                    preferred_element_type=jnp.float32,
                )
            for tile in range(tiles):
                strided_out[at[tile], :] = result[:, tile * 128 : (tile + 1) * 128]

        for tile in range(tiles):
            lanes = pl.ds(cs.start + tile * 128, 128)
            back_sent[leg, :, :, lanes] = (
                strided_out[pl.ds(tile * total, total), :]
                .astype(jnp.bfloat16)
                .reshape(bands, width, 128)
            )
        back = []
        for step in range(1, bands):
            band, where = band_at(step)
            back.append(
                send(
                    back_sent.at[leg, band, :, cs],
                    back_landed.at[leg, me, :, cs],
                    back_sem.at[leg, c, step - 1],
                    where,
                )
            )
        back_landed[leg, me, :, cs] = back_sent[leg, me, :, cs]
        return back

    def swap_back(leg, c, copies):
        cs = chunks[c]
        for copy in copies:
            copy.wait_recv()
        return send(
            back_landed.at[leg, :, :, cs], back_other.at[leg, :, :, cs], swap_sem.at[leg, c], mate
        )

    def to_grid_rows(base, target, leg, c, copy):
        cs = chunks[c]
        copy.wait_recv()

        @pl.loop(0, rows)
        def _(row):
            at = pl.ds(pl.multiple_of(row * per_row, per_row), per_row)
            near = back_landed[leg, :, at, cs].reshape(bands * per_row, -1)
            far = back_other[leg, :, at, cs].reshape(bands * per_row, -1)
            summed = jnp.dot(
                table_out[lon, lon], near, preferred_element_type=jnp.float32
            ) + jnp.dot(table_out[lon, 1 - lon], far, preferred_element_type=jnp.float32)
            moved = (base[row, :, cs].astype(jnp.float32) + summed * scale).astype(jnp.bfloat16)
            target[row, :, cs] = moved[: target.shape[1]]
            if leg == 0:
                term = jnp.dot(moved[:lons], win[cs, :], preferred_element_type=jnp.float32)
                pre_act[row] = term if c == 0 else pre_act[row] + term

    count = range(len(chunks))
    last = len(chunks) - 1
    field_pad[:, field_pad.shape[1] - 16 :, :] = jnp.zeros(
        (rows, 16, channels), field_pad.dtype
    )
    for row in range(rows):
        field_pad[row, :lons, :] = field[row]
    swaps = [swap_lon(field_pad, 0, c) for c in count]

    for place in range(8):
        strided_out[pl.ds(place, bands * modes, stride=8), :] = lax.dot_general(
            disco[...],
            cell_places[place],
            (((0,), (0,)), ((), ())),
            preferred_element_type=jnp.float32,
        )
    pieces[...] = (
        strided_out[: bands * modes * 8, :].reshape(pieces.shape).astype(jnp.bfloat16)
    )
    piece_copies = []
    for step in range(1, bands):
        band, where = band_at(step)
        piece_copies.append(
            send(pieces.at[band], pieces_all.at[me], piece_sem.at[step - 1], where)
        )
    pieces_all[me] = pieces[me]
    going = [to_owner(field_pad, 0, c, swaps[c]) for c in count]

    held = win_own.shape[0]
    mine = pl.ds(pl.multiple_of(chan * held, 16), held)
    beside = {"chan": 1 - chan}
    weight_copies = [
        send(wout_own, wout.at[mine], weight_sem.at[0], beside),
        send(win_own, win.at[mine], weight_sem.at[1], beside),
    ]
    win[mine, :] = win_own[...]
    wout[mine, :] = wout_own[...]
    gain[...] = gain_in[...].astype(jnp.float32)
    stack_parts(synthesis, analysis, right, left, to_pairs, to_eights)
    for copy in piece_copies:
        copy.wait_recv()
    pieces_f32[...] = pieces_all[...].astype(jnp.float32)

    coming = [spectral(0, c, going[c]) for c in count]
    for copy in weight_copies:
        copy.wait_recv()

    @pl.loop(0, rows)
    def _(row):
        grad_act[row] = lax.dot_general(
            cot[row], wout[...], (((1,), (1,)), ((), ())), preferred_element_type=jnp.float32
        )

    stack_parts(analysis, synthesis, left_t, right_t, to_eights, to_pairs)

    def finish(leg, base, target):
        swaps = [swap_back(leg, 0, coming[0])]
        for c in count:
            if c < last:
                swaps.append(swap_back(leg, c + 1, coming[c + 1]))
            to_grid_rows(base, target, leg, c, swaps[c])

    finish(0, field_pad, hidden)

    @pl.loop(0, rows)
    def _(row):
        grad_pre[row] = (grad_act[row] * gelu_slope(pre_act[row])).astype(jnp.bfloat16)

    swaps, going = [], []
    for c in count:
        cs = chunks[c]

        @pl.loop(0, rows)
        def _(row):
            back_rows = lax.dot_general(
                grad_pre[row],
                win[cs, :],
                (((1,), (1,)), ((), ())),
                preferred_element_type=jnp.float32,
            )
            hidden[row, :lons, cs] = (cot[row, :, cs].astype(jnp.float32) + back_rows).astype(
                jnp.bfloat16
            )

        swaps.append(swap_lon(hidden, 1, c))
        if c > 0:
            going.append(to_owner(hidden, 1, c - 1, swaps[c - 1]))
    going.append(to_owner(hidden, 1, last, swaps[last]))
    coming = [spectral(1, c, going[c]) for c in count]
    finish(1, hidden, out)
    for copy in started:
        copy.wait_send()


def per_device(
    field_in,
    cotangent,
    mlp_in_weight,
    mlp_out_weight,
    legendre_analysis,
    legendre_synthesis,
    spectral_gain,
    disco_filter,
    slot_pairs,
    slot_count,
):
    chans = lax.axis_size("chan")
    bands = lax.axis_size("lat") * chans
    lon_local, rows, channels = field_in.shape
    _, modes, degrees, all_rows = legendre_analysis.shape
    band = lax.axis_index(("lat", "chan"))
    lon_pad = -(-lon_local // 16) * 16

    slots = disco_filter.shape[0]
    lanes = -(-2 * all_rows // 128) * 128
    shape = (8, slots, 2, lanes)
    place, slot, piece, lane = (lax.broadcasted_iota(jnp.int32, shape, d) for d in range(4))
    slot_rows = slot_pairs[:, 0][None, :, None, None]
    slot_from = slot_rows + slot_pairs[:, 1][None, :, None, None] + (band * rows - REACH)
    part_out, part_in = place // rows, lane % 2
    met = (slot < slot_count[0]) & (place % rows == slot_rows) & (lane // 2 == slot_from)
    met = met & (place < 2 * rows) & (lane < 2 * all_rows) & ((part_out != part_in) == (piece == 1))
    sign = jnp.where(part_out < part_in, -1.0, 1.0)
    cell_places = jnp.where(met, sign, 0.0).astype(jnp.bfloat16).reshape(8, 2 * slots, lanes)

    own_rows = np.arange(all_rows)
    to_eights = np.zeros((2, bands * 8, all_rows), np.float32)
    to_pairs = np.zeros((2, 2 * all_rows, all_rows), np.float32)
    for part in range(2):
        to_eights[part, own_rows // rows * 8 + part * rows + own_rows % rows, own_rows] = 1.0
        to_pairs[part, 2 * own_rows + part, own_rows] = 1.0
    table = fixed_tables(bands, modes, lon_pad)

    chunks = tuple(pl.ds(start, size) for start, size in split_channels(channels))
    width = 2 * rows * modes
    widest = max(chunk.size for chunk in chunks) // 128
    held = (2, bands, width, channels)
    grid_shape = (rows, lon_pad, channels)
    out_shape = (rows, lon_local, channels)
    hidden_shape = (rows, lon_local, mlp_in_weight.shape[1])
    pieces_shape = (bands, modes * 8, lanes)
    bf16, f32 = jnp.bfloat16, jnp.float32
    vmem = pl.BlockSpec(memory_space=pltpu.VMEM)
    dma = pltpu.SemaphoreType.DMA
    result = pl.pallas_call(
        functools.partial(block_kernel, (bands, chans, rows, modes, channels, chunks)),
        out_shape=jax.ShapeDtypeStruct(out_shape, bf16),
        in_specs=[vmem] * 13,
        out_specs=vmem,
        scratch_shapes=[
            pltpu.VMEM(grid_shape, bf16),
            pltpu.VMEM((degrees, channels), f32),
            pltpu.VMEM((modes, 2 * degrees, bands * 8), bf16),
            pltpu.VMEM((modes, 2, 2 * all_rows, degrees), bf16),
            pltpu.VMEM((modes, 2, bands * 8, degrees), bf16),
            pltpu.VMEM((modes, 2 * degrees, 2 * all_rows), bf16),
            pltpu.VMEM(pieces_shape, bf16),
            pltpu.VMEM(hidden_shape, f32),
            pltpu.VMEM(hidden_shape, bf16),
            pltpu.VMEM((2,) + grid_shape, bf16),
            pltpu.VMEM(held, bf16),
            pltpu.VMEM(held, bf16),
            pltpu.VMEM(held, bf16),
            pltpu.VMEM(held, bf16),
            pltpu.VMEM(held, bf16),
            pltpu.VMEM(pieces_shape, bf16),
            pltpu.VMEM(pieces_shape, f32),
            pltpu.VMEM((widest * bands * width, 128), f32),
            pltpu.VMEM((widest * bands * width, 128), f32),
            pltpu.VMEM((channels, mlp_in_weight.shape[1]), bf16),
            pltpu.VMEM((mlp_out_weight.shape[0] * chans, channels), bf16),
            pltpu.VMEM(hidden_shape, f32),
            pltpu.VMEM(grid_shape, bf16),
            dma((2, len(chunks), 2)),
            dma((2, len(chunks), bands - 1, 2)),
            dma((2, len(chunks), bands - 1, 2)),
            dma((2, len(chunks), 2)),
            dma((bands - 1, 2)),
            dma((2, 2)),
        ],
        compiler_params=pltpu.CompilerParams(
            collective_id=0, has_side_effects=True, vmem_limit_bytes=56 * 1024 * 1024
        ),
    )(
        jnp.transpose(field_in, (1, 0, 2)),
        jnp.transpose(cotangent, (1, 0, 2)),
        mlp_in_weight,
        mlp_out_weight,
        disco_filter.reshape(2 * slots, bands * modes),
        cell_places,
        jnp.swapaxes(legendre_analysis[0], 1, 2),
        legendre_synthesis[0],
        jnp.asarray(to_eights, bf16),
        jnp.asarray(to_pairs, bf16),
        spectral_gain,
        jnp.asarray(table),
        jnp.asarray(table.transpose(1, 0, 3, 2)),
    )
    return jnp.transpose(result, (1, 0, 2))


def split_channels(channels):
    return [(start, min(256, channels - start)) for start in range(0, channels, 256)]


def solution(mesh):
    owned = MODES // (mesh.shape["lon"] * mesh.shape["lat"] * mesh.shape["chan"])
    fused = owned % 16 == 0 and mesh.shape["chan"] == 2 and mesh.shape["lon"] == 2
    return jax.shard_map(
        per_device if fused else per_device_plain,
        mesh=mesh,
        in_specs=(
            P(("groups", "lon"), ("lat", "chan"), None),
            P(("groups", "lon"), ("lat", "chan"), None),
            P("chan", None),
            P("chan", None),
            P("lon", ("lat", "chan"), None, None),
            P("lon", ("lat", "chan"), None, None),
            P(),
            P(("lat", "chan"), None, "lon"),
            P(("lat", "chan"), None),
            P(("lat", "chan")),
        ),
        out_specs=P(("groups", "lon"), ("lat", "chan"), None),
        check_vma=False,
    )
```

```python
import functools
import math

import jax
import jax.numpy as jnp
import numpy as np
from jax import lax
from jax.experimental import pallas as pl
from jax.experimental.pallas import tpu as pltpu
from jax.sharding import PartitionSpec as P

NLON = 720
MODES = 256
REACH = 2


def gelu_slope(inputs):
    normal_cdf = 0.5 * (1.0 + jax.scipy.special.erf(inputs * (1.0 / math.sqrt(2.0))))
    normal_pdf = jnp.exp(-0.5 * inputs * inputs) * (1.0 / math.sqrt(2.0 * math.pi))
    return normal_cdf + inputs * normal_pdf


def lon_tables(lon_ids, mode_ids):
    phase_index = lon_ids[:, None] * mode_ids[None, :] % NLON
    angle_rad = phase_index.astype(jnp.float32) * (2.0 * math.pi / NLON)
    return jnp.stack([jnp.cos(angle_rad), -jnp.sin(angle_rad)], axis=-1).astype(jnp.bfloat16)


def to_spectrum(grid_block):
    half_modes = MODES // lax.axis_size("lon")
    mode_ids = lax.axis_index("lon") * half_modes + jnp.arange(half_modes, dtype=jnp.int32)
    tail_shape = grid_block.shape[1:]
    piece_block = lax.all_gather(grid_block, "lon", axis=0, tiled=True)
    lon_count = piece_block.shape[0]
    lon_ids = jnp.arange(lon_count, dtype=jnp.int32)
    table_flat = lon_tables(lon_ids, mode_ids).reshape(lon_count, 2 * half_modes)
    summed = lax.dot_general(
        table_flat, piece_block, (((0,), (0,)), ((), ())), preferred_element_type=jnp.float32
    )
    return (
        (summed * (1.0 / math.sqrt(NLON)))
        .reshape((half_modes, 2) + tail_shape)
        .astype(jnp.bfloat16)
    )


def to_grid(band_block):
    lon_local = NLON // lax.axis_size("lon")
    lon_ids = lax.axis_index("lon") * lon_local + jnp.arange(lon_local, dtype=jnp.int32)
    tail_shape = band_block.shape[2:]
    piece_block = lax.all_gather(band_block, "lon", axis=0, tiled=True)
    mode_count = piece_block.shape[0]
    mode_ids = jnp.arange(mode_count, dtype=jnp.int32)
    table_flat = lon_tables(lon_ids, mode_ids).reshape(lon_local, 2 * mode_count)
    stacked = piece_block.reshape((2 * mode_count,) + tail_shape)
    summed = lax.dot_general(
        table_flat, stacked, (((1,), (0,)), ((), ())), preferred_element_type=jnp.float32
    )
    return summed * (1.0 / math.sqrt(NLON))


def to_owners(band_block):
    return lax.all_to_all(band_block, ("lat", "chan"), split_axis=0, concat_axis=2, tiled=True)


def to_bands(owned_block):
    return lax.all_to_all(owned_block, ("lat", "chan"), split_axis=2, concat_axis=0, tiled=True)


def band_filter(disco_filter, slot_pairs, slot_count, band_rows):
    width = 2 * REACH + 1
    in_use = jnp.arange(disco_filter.shape[0], dtype=jnp.int32) < slot_count[0]
    cell_of = slot_pairs[:, 0] * width + slot_pairs[:, 1]
    cells = jnp.arange(band_rows * width, dtype=jnp.int32)
    chosen = ((cells[:, None] == cell_of[None, :]) & in_use[None, :]).astype(jnp.bfloat16)
    return jnp.einsum(
        "ts,spk->tpk", chosen, disco_filter, preferred_element_type=jnp.float32
    ).astype(jnp.bfloat16)


def filter_matrices(cells, rows):
    width = 2 * REACH + 1
    by_row = cells.reshape(rows, width, 2, cells.shape[2])
    total = 0.0
    for offset in range(width):
        shifted = jnp.eye(rows, k=offset - REACH, dtype=jnp.bfloat16)
        total = total + jnp.transpose(by_row[:, offset], (2, 1, 0))[:, :, :, None] * shifted
    real, imag = total[:, 0], total[:, 1]
    return jnp.concatenate(
        [jnp.concatenate([real, -imag], axis=2), jnp.concatenate([imag, real], axis=2)], axis=1
    )


def per_device_plain(
    field_in,
    cotangent,
    mlp_in_weight,
    mlp_out_weight,
    legendre_analysis,
    legendre_synthesis,
    spectral_gain,
    disco_filter,
    slot_pairs,
    slot_count,
):
    analysis = legendre_analysis.reshape(legendre_analysis.shape[1:])
    synthesis = legendre_synthesis.reshape(legendre_synthesis.shape[1:])
    gain_table = spectral_gain.astype(jnp.float32)
    channels = field_in.shape[2]
    weight_in, weight_out = (
        lax.all_gather(mlp_in_weight, "chan", axis=0, tiled=True),
        lax.all_gather(mlp_out_weight, "chan", axis=0, tiled=True),
    )
    cells = band_filter(disco_filter, slot_pairs, slot_count, field_in.shape[1])
    modes_owned = analysis.shape[0]
    rows = analysis.shape[2]
    all_cells = lax.all_gather(cells, ("lat", "chan"), axis=0, tiled=True)
    own_cells = lax.dynamic_slice_in_dim(
        all_cells, lax.axis_index(("lat", "chan")) * modes_owned, modes_owned, 2
    )
    filters = filter_matrices(own_cells, rows)
    owned = to_owners(to_spectrum(field_in))
    mixed = (
        jnp.einsum(
            "kxy,kyc->kxc",
            filters,
            owned.reshape(modes_owned, 2 * rows, channels),
            preferred_element_type=jnp.float32,
        )
        .astype(jnp.bfloat16)
        .reshape(owned.shape)
    )
    coeffs = jnp.einsum("kla,krac->krlc", analysis, mixed, preferred_element_type=jnp.float32)
    filtered = (coeffs * gain_table).astype(jnp.bfloat16)
    synthesized = jnp.einsum(
        "kal,krlc->krac", synthesis, filtered, preferred_element_type=jnp.float32
    ).astype(jnp.bfloat16)
    spatial = to_grid(to_bands(synthesized))
    hidden_in = (field_in.astype(jnp.float32) + spatial).astype(jnp.bfloat16)
    hidden_rows = hidden_in.reshape(-1, channels)
    pre_act = jnp.dot(hidden_rows, weight_in, preferred_element_type=jnp.float32)
    grad_rows = cotangent.reshape(-1, channels)
    grad_act = lax.dot_general(
        grad_rows, weight_out, (((1,), (1,)), ((), ())), preferred_element_type=jnp.float32
    )
    grad_pre = (grad_act * gelu_slope(pre_act)).astype(jnp.bfloat16)
    back_rows = lax.dot_general(
        grad_pre, weight_in, (((1,), (1,)), ((), ())), preferred_element_type=jnp.float32
    )
    grad_hidden = (grad_rows.astype(jnp.float32) + back_rows).astype(jnp.bfloat16)
    grad_grid = grad_hidden.reshape(cotangent.shape)
    grad_owned = to_owners(to_spectrum(grad_grid))
    grad_coeffs = jnp.einsum(
        "kal,krac->krlc", synthesis, grad_owned, preferred_element_type=jnp.float32
    )
    grad_filtered = (grad_coeffs * gain_table).astype(jnp.bfloat16)
    grad_mixed = jnp.einsum(
        "kla,krlc->krac", analysis, grad_filtered, preferred_element_type=jnp.float32
    ).astype(jnp.bfloat16)
    grad_source = (
        jnp.einsum(
            "kxy,kxc->kyc",
            filters,
            grad_mixed.reshape(modes_owned, 2 * rows, channels),
            preferred_element_type=jnp.float32,
        )
        .astype(jnp.bfloat16)
        .reshape(grad_mixed.shape)
    )
    grad_spatial = to_grid(to_bands(grad_source))
    return (grad_grid.astype(jnp.float32) + grad_spatial).astype(jnp.bfloat16)


def fixed_tables(bands, modes, lon_pad):
    halves = MODES // (bands * modes)
    lon_ids = np.arange(NLON, dtype=np.int32)
    mode_ids = np.arange(MODES, dtype=np.int32)
    phase_index = lon_ids[:, None] * mode_ids[None, :] % NLON
    angle_rad = phase_index.astype(np.float32) * np.float32(2.0 * math.pi / NLON)
    paired = np.stack([np.cos(angle_rad), -np.sin(angle_rad)], axis=0)
    blocks = paired.reshape(2, halves, NLON // halves, halves, bands, modes)
    blocks = blocks.transpose(3, 1, 4, 0, 5, 2).reshape(halves, halves, bands * 2 * modes, -1)
    blocks = np.pad(blocks, ((0, 0), (0, 0), (0, 0), (0, lon_pad - blocks.shape[3])))
    return blocks.astype(jnp.bfloat16)


def block_kernel(
    sizes,
    field,
    cot,
    win_own,
    wout_own,
    disco,
    slot_pairs,
    slot_count,
    analysis,
    synthesis,
    to_eights,
    to_pairs,
    gain_in,
    table_in,
    table_out,
    out,
    field_pad,
    gain,
    left,
    right,
    left_t,
    right_t,
    pieces,
    pre_act,
    grad_pre,
    other,
    sent,
    landed,
    back_sent,
    back_landed,
    back_other,
    pieces_all,
    pieces_f32,
    strided_in,
    strided_out,
    win,
    wout,
    grad_act,
    hidden,
    lon_sem,
    go_sem,
    back_sem,
    swap_sem,
    piece_sem,
    weight_sem,
):
    bands, chans, rows, modes, channels, chunks = sizes
    width = 2 * rows * modes
    per_row = 2 * modes
    total = bands * width
    lat, chan, lon = lax.axis_index("lat"), lax.axis_index("chan"), lax.axis_index("lon")
    me = lat * chans + chan
    mate = {"lon": 1 - lon}
    lons = field.shape[1]
    scale = 1.0 / math.sqrt(NLON)
    started = []

    def band_at(step):
        band = lax.rem(me + step, bands)
        return band, {"lat": band // chans, "chan": lax.rem(band, chans)}

    def send(src, dst, sems, where):
        copy = pltpu.make_async_remote_copy(
            src_ref=src,
            dst_ref=dst,
            send_sem=sems.at[0],
            recv_sem=sems.at[1],
            device_id=where,
            device_id_type=pl.DeviceIdType.MESH,
        )
        copy.start()
        started.append(copy)
        return copy

    barrier = pltpu.get_barrier_semaphore()
    for step in range(1, bands):
        pl.semaphore_signal(
            barrier, inc=1, device_id=band_at(step)[1], device_id_type=pl.DeviceIdType.MESH
        )
    pl.semaphore_signal(barrier, inc=1, device_id=mate, device_id_type=pl.DeviceIdType.MESH)
    pl.semaphore_wait(barrier, bands)

    def swap_lon(source, leg, c):
        cs = chunks[c]
        return send(source.at[:, :, cs], other.at[leg, :, :, cs], lon_sem.at[leg, c], mate)

    def stack_parts(wide, tall, wide_ref, tall_ref, wide_places, tall_places):
        @pl.loop(0, modes, unroll=4)
        def _(mode):
            degrees = wide.shape[2]
            for part in range(2):
                wide_ref[mode, part] = jnp.dot(
                    wide_places[part], wide[mode], preferred_element_type=jnp.float32
                ).astype(jnp.bfloat16)
                tall_ref[mode, part * degrees : (part + 1) * degrees, :] = lax.dot_general(
                    tall[mode],
                    tall_places[part],
                    (((0,), (1,)), ((), ())),
                    preferred_element_type=jnp.float32,
                ).astype(jnp.bfloat16)

    def to_owner(source, leg, c, copy):
        cs = chunks[c]
        copy.wait_recv()

        @pl.loop(0, rows)
        def _(row):
            summed = jnp.dot(
                table_in[lon, lon], source[row, :, cs], preferred_element_type=jnp.float32
            ) + jnp.dot(
                table_in[lon, 1 - lon], other[leg, row, :, cs], preferred_element_type=jnp.float32
            )
            at = pl.ds(pl.multiple_of(row * per_row, per_row), per_row)
            sent[leg, :, at, cs] = (
                (summed * scale).astype(jnp.bfloat16).reshape(bands, per_row, -1)
            )

        copies = []
        for step in range(1, bands):
            band, where = band_at(step)
            copies.append(
                send(
                    sent.at[leg, band, :, cs],
                    landed.at[leg, me, :, cs],
                    go_sem.at[leg, c, step - 1],
                    where,
                )
            )
        landed[leg, me, :, cs] = sent[leg, me, :, cs]
        return copies

    def spectral(leg, c, copies):
        cs = chunks[c]
        tiles = cs.size // 128
        for copy in copies:
            copy.wait_recv()
        for tile in range(tiles):
            lanes = pl.ds(cs.start + tile * 128, 128)
            strided_in[pl.ds(tile * total, total), :] = (
                landed[leg, :, :, lanes].reshape(total, 128).astype(jnp.float32)
            )

        @pl.loop(0, modes, unroll=4)
        def _(mode):
            at = [pl.ds(tile * total + mode, 2 * rows * bands, stride=modes) for tile in range(tiles)]
            source = jnp.concatenate([strided_in[a, :] for a in at], axis=1).astype(jnp.bfloat16)
            eight = pl.ds(pl.multiple_of(mode * 8, 8), 8)
            filt = pieces_f32[:, eight, :].reshape(bands * 8, pieces_f32.shape[2])
            filt = filt[:, : 2 * rows * bands].astype(jnp.bfloat16)
            if leg == 0:
                source = jnp.dot(filt, source, preferred_element_type=jnp.float32)
                source = source.astype(jnp.bfloat16)
                first, second = left, right
            else:
                first, second = right_t, left_t
            coeffs = jnp.dot(first[mode], source, preferred_element_type=jnp.float32)
            degrees = coeffs.shape[0] // 2
            gained = (coeffs.reshape(2, degrees, -1) * gain[:, cs][None]).astype(jnp.bfloat16)
            result = jnp.dot(
                second[mode, 0], gained[0], preferred_element_type=jnp.float32
            ) + jnp.dot(second[mode, 1], gained[1], preferred_element_type=jnp.float32)
            if leg == 1:
                result = lax.dot_general(
                    filt,
                    result.astype(jnp.bfloat16),
                    (((0,), (0,)), ((), ())),
                    preferred_element_type=jnp.float32,
                )
            for tile in range(tiles):
                strided_out[at[tile], :] = result[:, tile * 128 : (tile + 1) * 128]

        for tile in range(tiles):
            lanes = pl.ds(cs.start + tile * 128, 128)
            back_sent[leg, :, :, lanes] = (
                strided_out[pl.ds(tile * total, total), :]
                .astype(jnp.bfloat16)
                .reshape(bands, width, 128)
            )
        back = []
        for step in range(1, bands):
            band, where = band_at(step)
            back.append(
                send(
                    back_sent.at[leg, band, :, cs],
                    back_landed.at[leg, me, :, cs],
                    back_sem.at[leg, c, step - 1],
                    where,
                )
            )
        back_landed[leg, me, :, cs] = back_sent[leg, me, :, cs]
        return back

    def swap_back(leg, c, copies):
        cs = chunks[c]
        for copy in copies:
            copy.wait_recv()
        return send(
            back_landed.at[leg, :, :, cs], back_other.at[leg, :, :, cs], swap_sem.at[leg, c], mate
        )

    def to_grid_rows(base, target, leg, c, copy):
        cs = chunks[c]
        copy.wait_recv()

        @pl.loop(0, rows)
        def _(row):
            at = pl.ds(pl.multiple_of(row * per_row, per_row), per_row)
            near = back_landed[leg, :, at, cs].reshape(bands * per_row, -1)
            far = back_other[leg, :, at, cs].reshape(bands * per_row, -1)
            summed = jnp.dot(
                table_out[lon, lon], near, preferred_element_type=jnp.float32
            ) + jnp.dot(table_out[lon, 1 - lon], far, preferred_element_type=jnp.float32)
            moved = (base[row, :, cs].astype(jnp.float32) + summed * scale).astype(jnp.bfloat16)
            target[row, :, cs] = moved[: target.shape[1]]
            if leg == 0:
                term = jnp.dot(moved[:lons], win[cs, :], preferred_element_type=jnp.float32)
                pre_act[row] = term if c == 0 else pre_act[row] + term

    count = range(len(chunks))
    last = len(chunks) - 1
    field_pad[:, field_pad.shape[1] - 16 :, :] = jnp.zeros(
        (rows, 16, channels), field_pad.dtype
    )
    for row in range(rows):
        field_pad[row, :lons, :] = field[row]
    swaps = [swap_lon(field_pad, 0, c) for c in count]

    slots, all_rows = slot_pairs.shape[1], bands * rows
    shape = (pieces.shape[2], slots)
    lane = lax.broadcasted_iota(jnp.int32, shape, 0)
    slot = lax.broadcasted_iota(jnp.int32, shape, 1)
    slot_rows = jnp.broadcast_to(slot_pairs[0:1, :], shape)
    slot_from = slot_rows + jnp.broadcast_to(slot_pairs[1:2, :], shape) + (me * rows - REACH)
    part_in = lane % 2
    met = (slot < slot_count[0]) & (lane // 2 == slot_from) & (lane < 2 * all_rows)
    for place in range(8):
        row_met = met & (slot_rows == place % rows) & (place < 2 * rows)
        total_rows = 0.0
        for piece in range(2):
            part_out = place // rows
            sign = jnp.where(part_in > part_out, -1.0, 1.0)
            part_met = (part_in == part_out) if piece == 0 else (part_in != part_out)
            cells = jnp.where(row_met & part_met, sign, 0.0).astype(jnp.bfloat16)
            total_rows = total_rows + lax.dot_general(
                disco[:, piece, :],
                cells,
                (((0,), (1,)), ((), ())),
                preferred_element_type=jnp.float32,
            )
        strided_out[pl.ds(place, bands * modes, stride=8), :] = total_rows
    pieces[...] = (
        strided_out[: bands * modes * 8, :].reshape(pieces.shape).astype(jnp.bfloat16)
    )
    piece_copies = []
    for step in range(1, bands):
        band, where = band_at(step)
        piece_copies.append(
            send(pieces.at[band], pieces_all.at[me], piece_sem.at[step - 1], where)
        )
    pieces_all[me] = pieces[me]
    going = [to_owner(field_pad, 0, c, swaps[c]) for c in count]

    held = win_own.shape[0]
    mine = pl.ds(pl.multiple_of(chan * held, 16), held)
    beside = {"chan": 1 - chan}
    weight_copies = [
        send(wout_own, wout.at[mine], weight_sem.at[0], beside),
        send(win_own, win.at[mine], weight_sem.at[1], beside),
    ]
    win[mine, :] = win_own[...]
    wout[mine, :] = wout_own[...]
    gain[...] = gain_in[...].astype(jnp.float32)
    stack_parts(synthesis, analysis, right, left, to_pairs, to_eights)
    for copy in piece_copies:
        copy.wait_recv()
    pieces_f32[...] = pieces_all[...].astype(jnp.float32)

    coming = [spectral(0, c, going[c]) for c in count]
    for copy in weight_copies:
        copy.wait_recv()

    @pl.loop(0, rows)
    def _(row):
        grad_act[row] = lax.dot_general(
            cot[row], wout[...], (((1,), (1,)), ((), ())), preferred_element_type=jnp.float32
        )

    stack_parts(analysis, synthesis, left_t, right_t, to_eights, to_pairs)

    def finish(leg, base, target):
        swaps = [swap_back(leg, 0, coming[0])]
        for c in count:
            if c < last:
                swaps.append(swap_back(leg, c + 1, coming[c + 1]))
            to_grid_rows(base, target, leg, c, swaps[c])

    finish(0, field_pad, hidden)

    @pl.loop(0, rows)
    def _(row):
        grad_pre[row] = (grad_act[row] * gelu_slope(pre_act[row])).astype(jnp.bfloat16)

    swaps, going = [], []
    for c in count:
        cs = chunks[c]

        @pl.loop(0, rows)
        def _(row):
            back_rows = lax.dot_general(
                grad_pre[row],
                win[cs, :],
                (((1,), (1,)), ((), ())),
                preferred_element_type=jnp.float32,
            )
            hidden[row, :lons, cs] = (cot[row, :, cs].astype(jnp.float32) + back_rows).astype(
                jnp.bfloat16
            )

        swaps.append(swap_lon(hidden, 1, c))
        if c > 0:
            going.append(to_owner(hidden, 1, c - 1, swaps[c - 1]))
    going.append(to_owner(hidden, 1, last, swaps[last]))
    coming = [spectral(1, c, going[c]) for c in count]
    finish(1, hidden, out)
    for copy in started:
        copy.wait_send()


def per_device(
    field_in,
    cotangent,
    mlp_in_weight,
    mlp_out_weight,
    legendre_analysis,
    legendre_synthesis,
    spectral_gain,
    disco_filter,
    slot_pairs,
    slot_count,
):
    chans = lax.axis_size("chan")
    bands = lax.axis_size("lat") * chans
    lon_local, rows, channels = field_in.shape
    _, modes, degrees, all_rows = legendre_analysis.shape
    lon_pad = -(-lon_local // 16) * 16

    lanes = -(-2 * all_rows // 128) * 128
    own_rows = np.arange(all_rows)
    to_eights = np.zeros((2, bands * 8, all_rows), np.float32)
    to_pairs = np.zeros((2, 2 * all_rows, all_rows), np.float32)
    for part in range(2):
        to_eights[part, own_rows // rows * 8 + part * rows + own_rows % rows, own_rows] = 1.0
        to_pairs[part, 2 * own_rows + part, own_rows] = 1.0
    table = fixed_tables(bands, modes, lon_pad)

    chunks = tuple(pl.ds(start, size) for start, size in split_channels(channels))
    width = 2 * rows * modes
    widest = max(chunk.size for chunk in chunks) // 128
    held = (2, bands, width, channels)
    grid_shape = (rows, lon_pad, channels)
    out_shape = (rows, lon_local, channels)
    hidden_shape = (rows, lon_local, mlp_in_weight.shape[1])
    pieces_shape = (bands, modes * 8, lanes)
    bf16, f32 = jnp.bfloat16, jnp.float32
    vmem = pl.BlockSpec(memory_space=pltpu.VMEM)
    dma = pltpu.SemaphoreType.DMA
    result = pl.pallas_call(
        functools.partial(block_kernel, (bands, chans, rows, modes, channels, chunks)),
        out_shape=jax.ShapeDtypeStruct(out_shape, bf16),
        in_specs=[vmem] * 6 + [pl.BlockSpec(memory_space=pltpu.SMEM)] + [vmem] * 7,
        out_specs=vmem,
        scratch_shapes=[
            pltpu.VMEM(grid_shape, bf16),
            pltpu.VMEM((degrees, channels), f32),
            pltpu.VMEM((modes, 2 * degrees, bands * 8), bf16),
            pltpu.VMEM((modes, 2, 2 * all_rows, degrees), bf16),
            pltpu.VMEM((modes, 2, bands * 8, degrees), bf16),
            pltpu.VMEM((modes, 2 * degrees, 2 * all_rows), bf16),
            pltpu.VMEM(pieces_shape, bf16),
            pltpu.VMEM(hidden_shape, f32),
            pltpu.VMEM(hidden_shape, bf16),
            pltpu.VMEM((2,) + grid_shape, bf16),
            pltpu.VMEM(held, bf16),
            pltpu.VMEM(held, bf16),
            pltpu.VMEM(held, bf16),
            pltpu.VMEM(held, bf16),
            pltpu.VMEM(held, bf16),
            pltpu.VMEM(pieces_shape, bf16),
            pltpu.VMEM(pieces_shape, f32),
            pltpu.VMEM((widest * bands * width, 128), f32),
            pltpu.VMEM((widest * bands * width, 128), f32),
            pltpu.VMEM((channels, mlp_in_weight.shape[1]), bf16),
            pltpu.VMEM((mlp_out_weight.shape[0] * chans, channels), bf16),
            pltpu.VMEM(hidden_shape, f32),
            pltpu.VMEM(grid_shape, bf16),
            dma((2, len(chunks), 2)),
            dma((2, len(chunks), bands - 1, 2)),
            dma((2, len(chunks), bands - 1, 2)),
            dma((2, len(chunks), 2)),
            dma((bands - 1, 2)),
            dma((2, 2)),
        ],
        compiler_params=pltpu.CompilerParams(
            collective_id=0, has_side_effects=True, vmem_limit_bytes=56 * 1024 * 1024
        ),
    )(
        jnp.transpose(field_in, (1, 0, 2)),
        jnp.transpose(cotangent, (1, 0, 2)),
        mlp_in_weight,
        mlp_out_weight,
        disco_filter,
        jnp.transpose(slot_pairs),
        slot_count,
        jnp.swapaxes(legendre_analysis[0], 1, 2),
        legendre_synthesis[0],
        jnp.asarray(to_eights, bf16),
        jnp.asarray(to_pairs, bf16),
        spectral_gain,
        jnp.asarray(table),
        jnp.asarray(table.transpose(1, 0, 3, 2)),
    )
    return jnp.transpose(result, (1, 0, 2))


def split_channels(channels):
    return [(start, min(256, channels - start)) for start in range(0, channels, 256)]


def solution(mesh):
    owned = MODES // (mesh.shape["lon"] * mesh.shape["lat"] * mesh.shape["chan"])
    fused = owned % 16 == 0 and mesh.shape["chan"] == 2 and mesh.shape["lon"] == 2
    return jax.shard_map(
        per_device if fused else per_device_plain,
        mesh=mesh,
        in_specs=(
            P(("groups", "lon"), ("lat", "chan"), None),
            P(("groups", "lon"), ("lat", "chan"), None),
            P("chan", None),
            P("chan", None),
            P("lon", ("lat", "chan"), None, None),
            P("lon", ("lat", "chan"), None, None),
            P(),
            P(("lat", "chan"), None, "lon"),
            P(("lat", "chan"), None),
            P(("lat", "chan")),
        ),
        out_specs=P(("groups", "lon"), ("lat", "chan"), None),
        check_vma=False,
    )
```
